128 devices in a mesh: heads: 8 (over z_hi, x), ctx: 16 (over y, z_lo, core).
Axes of the slice: x: 4, y: 4, z: 4 (z_hi: 2, z_lo: 2; z = z_hi * 2 + z_lo), core: 2. Of those that a mesh axis runs over, the one named last changes fastest.
Arguments:
- queries: bfloat16 [16384, 8192], P('ctx', 'heads'), may hold values from -6 to 6
- keys: bfloat16 [16384, 1024], P('ctx', 'heads'), may hold values from -6 to 6
- values: bfloat16 [16384, 1024], P('ctx', 'heads'), may hold values from -6 to 6
- outputs: bfloat16 [16384, 8192], P('ctx', 'heads'), may hold values from -6 to 6
- out_grad: bfloat16 [16384, 5120], P('ctx', 'heads'), may hold values from -6 to 6
- out_weight: bfloat16 [8192, 5120], P('heads'), may hold values from -0.0625 to 0.0625
- log_norm: float32 [64, 16384], P('heads', 'ctx'), may hold values from 4 to 8
- doc_ids: int32 [16384], replicated, may hold values from 0 to 31, as said below
Outputs:
- grad_queries: bfloat16 [16384, 8192], P('ctx', 'heads')
- grad_keys: bfloat16 [16384, 1024], P('ctx', 'heads')
- grad_values: bfloat16 [16384, 1024], P('ctx', 'heads')
The draws below stay inside these ranges and needn't reach their ends.
Inputs may be any that keep to these rules, and one draw needn't show every extreme that they name: `doc_ids`: document numbers never fall along the sequence; document 0 starts at token 0 and document k, for k of 1 or more, starts strictly inside the k-th half of a sequence block (tokens k * 512 + 1 onward, before (k + 1) * 512).
All inputs are finite; a program needn't handle non-finite values.
Results may differ from the reference program's by a relative error of at most 0.02.
Values may be sent and summed in bfloat16 or wider, within the bound.
A program may use at most 192 MiB of HBM per device.

```python
import math
import jax
import jax.numpy as jnp
from jax import lax

D = 5120
HD = 128
GROUP = 8
KVHEADS = 8
QHEADS = 64
TOK_DEV = 1024
WIN_BLOCKS = 1
TOKENS = 16384
DOCS = 32


def draw_doc_ids(key, part):
    key = jax.random.fold_in(key, 5)
    half_len = TOK_DEV // 2
    shifts = jax.random.randint(key, (DOCS,), 1, half_len, dtype=jnp.int32)
    doc_index = jnp.arange(DOCS, dtype=jnp.int32)
    starts = doc_index * half_len + shifts
    tokens_at = jnp.arange(TOKENS, dtype=jnp.int32)
    later = (tokens_at[:, None] >= starts[None, 1:]).astype(jnp.int32)
    return jnp.sum(later, axis=1).astype(jnp.int32)


def level_of(stream_key, shape, pieces, least, top_value):
    factor_of, own = 1.0, jax.random.fold_in(stream_key, 6)
    for dim, shards_of in pieces:
        draws = jnp.exp(jax.random.uniform(jax.random.fold_in(own, dim), (shards_of,), jnp.float32, least / len(pieces), top_value / len(pieces)))
        factor_of = factor_of * jnp.repeat(draws, shape[dim] // shards_of).reshape([-1 if axis == dim else 1 for axis in range(len(shape))])
    return factor_of


def normal_values(key, extent, scale, bound, cuts=(), kind=jnp.bfloat16):
    factor_of = level_of(key, extent, cuts, -0.22, 0.18) if cuts else 1.0
    drawn = jax.random.normal(key, extent, jnp.float32) * scale * factor_of
    return jnp.minimum(jnp.maximum(drawn, -bound), bound).astype(kind)


def setup_inputs(seed: int = 0) -> dict:
    key_of = jax.random.split(jax.random.key(seed), 9)
    queries = normal_values(key_of[0], (TOKENS, QHEADS * HD), 1.0, 6.0, ((0, 16), (1, 8)))
    keys = normal_values(key_of[1], (TOKENS, KVHEADS * HD), 1.0, 6.0, ((0, 16), (1, 8)))
    values = normal_values(key_of[2], (TOKENS, KVHEADS * HD), 1.0, 6.0, ((0, 16), (1, 8)))
    outputs = normal_values(key_of[3], (TOKENS, QHEADS * HD), 1.0, 6.0, ((0, 16), (1, 8)))
    out_grad = normal_values(key_of[4], (TOKENS, D), 1.0, 6.0, ((0, 16), (1, 8)))
    out_weight = normal_values(key_of[5], (QHEADS * HD, D), (QHEADS * HD) ** -0.5, 0.0625, ((0, 8),))
    log_norm = jnp.clip(4.0 + 4.0 * jax.random.uniform(key_of[6], (QHEADS, TOKENS), jnp.float32) ** level_of(key_of[6], (QHEADS, TOKENS), ((0, 8), (1, 16)), -0.2, 0.2), 4.0, 8.0)
    doc_ids = draw_doc_ids(jax.random.fold_in(key_of[8], 71), 0)
    return {"queries": queries, "keys": keys, "values": values, "outputs": outputs, "out_grad": out_grad, "out_weight": out_weight, "log_norm": log_norm, "doc_ids": doc_ids}


def reference(queries, keys, values, outputs, out_grad, out_weight, log_norm, doc_ids):
    length = queries.shape[0]
    kv_heads = keys.shape[1] // HD
    blocks = length // TOK_DEV
    window = WIN_BLOCKS * TOK_DEV
    span = TOK_DEV + window
    softmax_scale = 1.0 / math.sqrt(HD)
    grad_out = jnp.dot(out_grad, out_weight.T, preferred_element_type=jnp.float32).astype(jnp.bfloat16)
    query_all = queries.reshape(blocks, TOK_DEV, kv_heads, GROUP, HD).transpose(2, 0, 1, 3, 4)
    grad_all = grad_out.reshape(blocks, TOK_DEV, kv_heads, GROUP, HD).transpose(2, 0, 1, 3, 4)
    delta_all = lax.optimization_barrier(jnp.sum((grad_out.astype(jnp.float32) * outputs.astype(jnp.float32)).reshape(length, kv_heads, GROUP, HD), axis=-1))
    delta_all = delta_all.reshape(blocks, TOK_DEV, kv_heads, GROUP).transpose(2, 0, 3, 1)
    lse_all = log_norm.reshape(kv_heads, GROUP, blocks, TOK_DEV).transpose(0, 2, 1, 3)
    key_all = keys.reshape(length, kv_heads, HD).transpose(1, 0, 2)
    value_all = values.reshape(length, kv_heads, HD).transpose(1, 0, 2)
    positions = jnp.arange(length, dtype=jnp.int32)
    pad_pos = jnp.arange(length + window, dtype=jnp.int32) - window
    pad_doc = jnp.concatenate([jnp.full((window,), -1, jnp.int32), doc_ids.astype(jnp.int32)])
    query_pos = positions.reshape(blocks, TOK_DEV)
    query_doc = doc_ids.reshape(blocks, TOK_DEV)
    block_ids = jnp.arange(blocks, dtype=jnp.int32)

    def one_head(packed):
        query_h, grad_h, delta_h, lse_h, key_h, value_h = packed
        front = jnp.zeros((window, HD), jnp.float32)
        key_pad = jnp.concatenate([front, key_h.astype(jnp.float32)], axis=0)
        value_pad = jnp.concatenate([front, value_h.astype(jnp.float32)], axis=0)

        def one_block(carry, items):
            key_acc, value_acc = carry
            query_b, grad_b, delta_b, lse_b, pos_b, doc_b, block_b = items
            start = (block_b * TOK_DEV).astype(jnp.int32)
            key_f = lax.dynamic_slice_in_dim(key_pad, start, span, 0)
            value_f = lax.dynamic_slice_in_dim(value_pad, start, span, 0)
            key_pos = lax.dynamic_slice_in_dim(pad_pos, start, span, 0)
            key_doc = lax.dynamic_slice_in_dim(pad_doc, start, span, 0)
            allowed = (doc_b[:, None] == key_doc[None, :]) & (key_pos[None, :] <= pos_b[:, None]) & (key_pos[None, :] > pos_b[:, None] - window)
            query_f = query_b.astype(jnp.float32)
            grad_f = grad_b.astype(jnp.float32)
            scores = jnp.einsum('qgd,kd->gqk', query_f, key_f) * softmax_scale
            probs = jnp.where(allowed[None], jnp.exp(scores - lse_b[:, :, None]), jnp.float32(0.0))
            dprobs = jnp.einsum('qgd,kd->gqk', grad_f, value_f)
            dscores = probs * (dprobs - delta_b[:, :, None])
            probs_low = probs.astype(jnp.bfloat16).astype(jnp.float32)
            dscores_low = dscores.astype(jnp.bfloat16).astype(jnp.float32)
            value_term = jnp.einsum('gqk,qgd->kd', probs_low, grad_f)
            key_term = jnp.einsum('gqk,qgd->kd', dscores_low, query_f) * softmax_scale
            query_grad = jnp.einsum('gqk,kd->qgd', dscores_low, key_f) * softmax_scale
            value_acc = lax.dynamic_update_slice_in_dim(value_acc, lax.dynamic_slice_in_dim(value_acc, start, span, 0) + value_term, start, 0)
            key_acc = lax.dynamic_update_slice_in_dim(key_acc, lax.dynamic_slice_in_dim(key_acc, start, span, 0) + key_term, start, 0)
            return ((key_acc, value_acc), query_grad)
        zeros = jnp.zeros((length + window, HD), jnp.float32)
        (key_acc, value_acc), query_grads = lax.scan(one_block, (zeros, zeros), (query_h, grad_h, delta_h, lse_h, query_pos, query_doc, block_ids))
        return (query_grads, key_acc[window:], value_acc[window:])
    query_grads, key_grads, value_grads = lax.map(one_head, (query_all, grad_all, delta_all, lse_all, key_all, value_all))
    grad_queries = query_grads.transpose(1, 2, 0, 3, 4).reshape(length, kv_heads * GROUP * HD).astype(jnp.bfloat16)
    grad_keys = key_grads.transpose(1, 0, 2).reshape(length, kv_heads * HD).astype(jnp.bfloat16)
    grad_values = value_grads.transpose(1, 0, 2).reshape(length, kv_heads * HD).astype(jnp.bfloat16)
    return (grad_queries, grad_keys, grad_values)
```

```python
import functools
import math

import jax
import jax.numpy as jnp
from jax import lax
from jax.experimental import pallas as pl
from jax.experimental.pallas import tpu as pltpu
from jax.sharding import PartitionSpec as P

MESH = pl.DeviceIdType.MESH
TOK = 1024
HALF = 512
HD = 128
GROUP = 8
COLS = 640
D = 5120
QT = 256
ROWS = 64
CHUNKS = TOK // ROWS
PER_TILE = QT // ROWS
FLOWS = 8
LOG2E = math.log2(math.e)
NT = (((1,), (1,)), ((), ()))
NN = (((1,), (0,)), ((), ()))


def dot(a, b, dims):
    return lax.dot_general(a, b, dims, preferred_element_type=jnp.float32)


def kernel(
    q_hbm, k_hbm, v_hbm, o_hbm, og_hbm, w_hbm, lse_ref, doc_ref,
    dq_ref, dk_ref, dv_ref,
    gat, wv, qv, ov, ot, key, val, key_t, dk_acc, dv_acc, dk_in, dv_in, bias, doc_col, doc_row,
    send, recv, kv_send, kv_recv, back_send, back_recv, load,
):
    heads = lax.axis_index("heads")
    ctx = lax.axis_index("ctx")
    n_ctx = lax.axis_size("ctx")
    plane, x = heads // 4, heads % 4
    x_left, x_right, x_far = (x + 3) % 4, (x + 1) % 4, (x + 2) % 4
    other = 1 - plane
    right = {"heads": plane * 4 + x_right}
    left = {"heads": plane * 4 + x_left}
    across = {"heads": other * 4 + x}
    after = {"ctx": (ctx + 1) % n_ctx}
    before = {"ctx": (ctx + n_ctx - 1) % n_ctx}

    def cell(pl_, x_, row, rows):
        col = pl.multiple_of((pl_ * 4 + x_) * COLS, 128)
        return gat.at[pl.ds(row, rows), pl.ds(col, COLS)]

    def flow(f, j, received=False):
        r0 = pl.multiple_of(j * ROWS, ROWS)
        hr = ROWS // 2
        if f < 3:
            to = (right, left, across)[f]
            mine = cell(plane, x, r0, ROWS)
            src = og_hbm.at[pl.ds(r0, ROWS), :]
            got = (cell(plane, x_left, r0, ROWS), cell(plane, x_right, r0, ROWS), cell(other, x, r0, ROWS))[f]
        elif f == 3:
            to = right
            mine = src = cell(plane, x_left, r0, hr)
            got = cell(plane, x_far, r0, hr)
        elif f == 4:
            to = left
            mine = src = cell(plane, x_right, r0 + hr, hr)
            got = cell(plane, x_far, r0 + hr, hr)
        elif f in (5, 6):
            to = (right, left)[f - 5]
            mine = src = cell(other, x, r0, ROWS)
            got = cell(other, (x_left, x_right)[f - 5], r0, ROWS)
        else:
            to = across
            mine = src = cell(plane, x_far, r0, ROWS)
            got = cell(other, x_far, r0, ROWS)
        dst = mine
        if received:
            src = dst = got
        return pltpu.make_async_remote_copy(
            src_ref=src, dst_ref=dst, send_sem=send.at[f, j], recv_sem=recv.at[f, j],
            device_id=to, device_id_type=MESH,
        )

    def start(f, j):
        flow(f, j).start()

    def arrived(f, j):
        flow(f, j, received=True).wait_recv()

    def own(j):
        for f in range(3):
            start(f, j)

    def stage_a(j):
        arrived(0, j)
        start(3, j)
        arrived(1, j)
        start(4, j)
        arrived(2, j)
        start(5, j)
        start(6, j)

    def stage_b(j):
        arrived(3, j)
        arrived(4, j)
        start(7, j)

    def stage_c(j):
        for f in (5, 6, 7):
            arrived(f, j)

    def slot(t):
        @pl.when(t + 4 < CHUNKS)
        def _():
            own(t + 4)

        @pl.when(t + 2 < CHUNKS)
        def _():
            stage_a(t + 2)

        @pl.when(t + 1 < CHUNKS)
        def _():
            stage_b(t + 1)

        stage_c(t)

    def kv_copy(i, received=False):
        buf = (key, val)[i]
        src = (k_hbm, v_hbm)[i].at[pl.ds(HALF, HALF), :]
        dst = buf.at[pl.ds(0, HALF), :]
        return pltpu.make_async_remote_copy(
            src_ref=src, dst_ref=dst, send_sem=kv_send.at[i], recv_sem=kv_recv.at[i],
            device_id=after, device_id_type=MESH,
        )

    def back_copy(i):
        return pltpu.make_async_remote_copy(
            src_ref=(dk_acc, dv_acc)[i].at[pl.ds(0, HALF), :], dst_ref=(dk_in, dv_in)[i],
            send_sem=back_send.at[i], recv_sem=back_recv.at[i],
            device_id=before, device_id_type=MESH,
        )

    loads = [
        pltpu.make_async_copy(k_hbm, key.at[pl.ds(HALF, TOK), :], load.at[0]),
        pltpu.make_async_copy(v_hbm, val.at[pl.ds(HALF, TOK), :], load.at[1]),
        pltpu.make_async_copy(o_hbm, ov, load.at[2]),
        pltpu.make_async_copy(og_hbm, cell(plane, x, 0, TOK), load.at[3]),
        pltpu.make_async_copy(q_hbm, qv, load.at[4]),
        pltpu.make_async_copy(w_hbm, wv, load.at[5]),
    ]
    for c in loads:
        c.start()

    barrier = pltpu.get_barrier_semaphore()
    for d in (right, left, across, after, before):
        pl.semaphore_signal(barrier, inc=1, device_id=d, device_id_type=MESH)
    pl.semaphore_wait(barrier, 5)
    for j in range(4):
        own(j)
    for i in range(2):
        kv_copy(i).start()

    dk_acc[...] = jnp.zeros_like(dk_acc)
    dv_acc[...] = jnp.zeros_like(dv_acc)
    half = ctx * 2
    n_half = n_ctx * 2
    for b in range(3):
        docs = doc_ref[(half + n_half - 1 + b) % n_half].astype(jnp.float32)
        doc_row[:, b * HALF:(b + 1) * HALF] = docs
        doc_col[b * HALF:(b + 1) * HALF, :] = jnp.broadcast_to(docs, (128, HALF)).T

    loads[0].wait()
    loads[1].wait()
    key_t[:, HALF:] = key[HALF:, :].T
    loads[2].wait()

    def turn(h, carry):
        c0 = pl.multiple_of(h * HD, HD)
        ot[pl.ds(c0, HD), :] = ov[:, pl.ds(c0, HD)].T
        return carry

    stage_a(0)
    lax.fori_loop(0, GROUP, turn, 0)
    for c in loads[3:]:
        c.wait()
    stage_a(1)
    stage_b(0)
    for i in range(2):
        kv_copy(i).wait_recv()
    key_t[:, :HALF] = key[:HALF, :].T

    scale = 1.0 / math.sqrt(HD)

    def set_bias(i):
        k0, kk = (i // 2) * HALF, 768 + (i % 2) * QT
        q0 = HALF + i * QT
        row = doc_row[:, q0:q0 + QT]
        for part in range(kk // QT):
            lo = k0 + part * QT
            col = doc_col[lo:lo + QT, :]
            same = jnp.concatenate([col, col], axis=1) == row
            if lo == q0:
                kp = lax.broadcasted_iota(jnp.int32, (QT, QT), 0)
                qp = lax.broadcasted_iota(jnp.int32, (QT, QT), 1)
                same = same & (kp <= qp)
            bias[part * QT:(part + 1) * QT, :] = jnp.where(same, 0.0, -1e30)

    def piece(i, hp):
        k0, kk = (i // 2) * HALF, 768 + (i % 2) * QT
        r0 = i * QT
        f0 = pl.multiple_of(hp * 2 * HD, 2 * HD)
        got = dot(wv[pl.ds(f0, 2 * HD), :], gat[r0:r0 + QT, :], NT).astype(jnp.bfloat16)
        for a in range(2):
            h = hp * 2 + a
            c0 = pl.multiple_of(h * HD, HD)
            g = got[a * HD:(a + 1) * HD]
            q = qv[r0:r0 + QT, pl.ds(c0, HD)]
            o = ot[pl.ds(c0, HD), r0:r0 + QT]
            delta = jnp.sum(g.astype(jnp.float32) * o.astype(jnp.float32), axis=0, keepdims=True)
            lse = lse_ref[pl.ds(h, 1), r0:r0 + QT] * LOG2E
            kb = key[k0:k0 + kk, :]
            s = dot(kb, q, NT)
            p = jnp.exp2((s * (scale * LOG2E) - lse) + bias[:kk, :])
            dp = dot(val[k0:k0 + kk, :], g, NN)
            ds = (p * (dp - delta)).astype(jnp.bfloat16)
            dv_acc[k0:k0 + kk, :] += dot(p.astype(jnp.bfloat16), g, NT)
            dk_acc[k0:k0 + kk, :] += dot(ds, q, NN)
            dq_t = dot(key_t[:, k0:k0 + kk], ds, NN) * scale
            dq_ref[r0:r0 + QT, pl.ds(c0, HD)] = dq_t.T.astype(jnp.bfloat16)

    def step(t, carry):
        slot(t)
        return carry

    lax.fori_loop(0, PER_TILE, step, 0)
    for i in range(TOK // QT):
        set_bias(i)

        def body(hp, carry, i=i):
            if i + 1 < TOK // QT:
                slot((i + 1) * PER_TILE + hp)
            piece(i, hp)
            return carry

        lax.fori_loop(0, PER_TILE, body, 0)
        if i == 1:
            for b in range(2):
                back_copy(b).start()

    for b in range(2):
        back_copy(b).wait()
        kv_copy(b).wait_send()

    def drain(j, carry):
        for f in range(FLOWS):
            flow(f, j).wait_send()
        return carry

    lax.fori_loop(0, CHUNKS, drain, 0)
    dk_ref[:HALF, :] = (dk_acc[HALF:TOK, :] * scale).astype(jnp.bfloat16)
    dk_ref[HALF:, :] = ((dk_acc[TOK:, :] + dk_in[...]) * scale).astype(jnp.bfloat16)
    dv_ref[:HALF, :] = dv_acc[HALF:TOK, :].astype(jnp.bfloat16)
    dv_ref[HALF:, :] = (dv_acc[TOK:, :] + dv_in[...]).astype(jnp.bfloat16)


def per_device(queries, keys, values, outputs, out_grad, out_weight, log_norm, doc_ids):
    bf, f32 = jnp.bfloat16, jnp.float32
    any_ = pl.BlockSpec(memory_space=pl.ANY)
    vm = pl.BlockSpec(memory_space=pltpu.VMEM)
    dma = pltpu.SemaphoreType.DMA
    wide = HALF + TOK
    return pl.pallas_call(
        kernel,
        out_shape=(
            jax.ShapeDtypeStruct((TOK, GROUP * HD), bf),
            jax.ShapeDtypeStruct((TOK, HD), bf),
            jax.ShapeDtypeStruct((TOK, HD), bf),
        ),
        in_specs=[any_] * 6 + [vm] * 2,
        out_specs=(vm, vm, vm),
        scratch_shapes=[
            pltpu.VMEM((TOK, D), bf),
            pltpu.VMEM((GROUP * HD, D), bf),
            pltpu.VMEM((TOK, GROUP * HD), bf),
            pltpu.VMEM((TOK, GROUP * HD), bf),
            pltpu.VMEM((GROUP * HD, TOK), bf),
            pltpu.VMEM((wide, HD), bf),
            pltpu.VMEM((wide, HD), bf),
            pltpu.VMEM((HD, wide), bf),
            pltpu.VMEM((wide, HD), f32),
            pltpu.VMEM((wide, HD), f32),
            pltpu.VMEM((HALF, HD), f32),
            pltpu.VMEM((HALF, HD), f32),
            pltpu.VMEM((TOK, QT), f32),
            pltpu.VMEM((wide, 128), f32),
            pltpu.VMEM((1, wide), f32),
            dma((FLOWS, CHUNKS)),
            dma((FLOWS, CHUNKS)),
            dma((2,)), dma((2,)), dma((2,)), dma((2,)), dma((6,)),
        ],
        compiler_params=pltpu.CompilerParams(
            collective_id=0, has_side_effects=True, vmem_limit_bytes=58 * 2**20
        ),
        name="attention_backward",
    )(queries, keys, values, outputs, out_grad, out_weight, log_norm, doc_ids.reshape(32, 1, HALF))


def solution(mesh):
    in_specs = (
        P("ctx", "heads"), P("ctx", "heads"), P("ctx", "heads"), P("ctx", "heads"), P("ctx", "heads"),
        P("heads", None), P("heads", "ctx"), P(),
    )
    out_specs = (P("ctx", "heads"), P("ctx", "heads"), P("ctx", "heads"))
    return jax.shard_map(per_device, mesh=mesh, in_specs=in_specs, out_specs=out_specs, check_vma=False)
```

```python
import functools
import math

import jax
import jax.numpy as jnp
from jax import lax
from jax.experimental import pallas as pl
from jax.experimental.pallas import tpu as pltpu
from jax.sharding import PartitionSpec as P

MESH = pl.DeviceIdType.MESH
TOK = 1024
HALF = 512
HD = 128
GROUP = 8
COLS = 640
D = 5120
LEADS = (3, 3, 2, 5)
PARTS = ((0, 128), (128, 128), (256, 128), (384, 128), (768, 128), (896, 128), (640, 128), (512, 128))
CHUNKS = len(PARTS)
EDGE = 16
TILES = ((0, 256), (256, 256), (768, 256), (640, 128), (512, 128))
NEED = (1, 3, 5, 6, 7)
FIRST = 1
EDGED = 2
FLOWS = 10
LOG2E = math.log2(math.e)
NT = (((1,), (1,)), ((), ()))
NN = (((1,), (0,)), ((), ()))
FROWS = 256


def dot(a, b, dims):
    return lax.dot_general(a, b, dims, preferred_element_type=jnp.float32)


def kernel(
    q_hbm, k_hbm, v_hbm, o_hbm, og_hbm, w_hbm, lse_ref, doc_ref,
    dq_hbm, dk_ref, dv_ref,
    dq_ref, gt, gat, wv, qv, ov, ot, key, val, key_t, dk_acc, dv_acc, dk_in, dv_in, dk_out, dv_out, part, p_wide, p_slim, bias, doc_col, doc_row,
    send, recv, kv_send, kv_recv, back_send, back_recv, load, store,
):
    heads = lax.axis_index("heads")
    ctx = lax.axis_index("ctx")
    n_ctx = lax.axis_size("ctx")
    plane, x = heads // 4, heads % 4
    x_left, x_right, x_far = (x + 3) % 4, (x + 1) % 4, (x + 2) % 4
    other = 1 - plane
    right = {"heads": plane * 4 + x_right}
    left = {"heads": plane * 4 + x_left}
    across = {"heads": other * 4 + x}
    after = {"ctx": (ctx + 1) % n_ctx}
    before = {"ctx": (ctx + n_ctx - 1) % n_ctx}

    def cell(pl_, x_, row, rows):
        col = pl.multiple_of((pl_ * 4 + x_) * COLS, 128)
        return gat.at[pl.ds(row, rows), pl.ds(col, COLS)]

    def flow(f, j, received=False):
        r0, rows = PARTS[j]
        low, hr = rows - EDGE * (j < EDGED), rows // 2
        to = (right, left, across, right, left, right, left, across, across, across)[f]
        first, rows = (
            (r0, rows), (r0, rows), (r0, rows), (r0, hr), (r0 + hr, hr),
            (r0, low), (r0, low), (r0, rows), (r0 + low, EDGE), (r0 + low, EDGE),
        )[f]
        sent = (
            (plane, x), (plane, x), (plane, x), (plane, x_left), (plane, x_right),
            (other, x), (other, x), (plane, x_far), (plane, x_left), (plane, x_right),
        )[f]
        filled = (
            (plane, x_left), (plane, x_right), (other, x), (plane, x_far), (plane, x_far),
            (other, x_left), (other, x_right), (other, x_far), (other, x_left), (other, x_right),
        )[f]
        dst = cell(*(filled if received else sent), first, rows)
        src = og_hbm.at[pl.ds(first, rows), :] if f < 3 and not received else dst
        return pltpu.make_async_remote_copy(
            src_ref=src, dst_ref=dst, send_sem=send.at[f, j], recv_sem=recv.at[f, j],
            device_id=to, device_id_type=MESH,
        )

    def start(f, j):
        if f < 8 or j < EDGED:
            flow(f, j).start()

    def arrived(f, j):
        if f < 8 or j < EDGED:
            flow(f, j, received=True).wait_recv()

    def own(j):
        for f in range(3):
            start(f, j)

    def near(j):
        arrived(0, j)
        start(3, j)
        start(8, j)
        arrived(1, j)
        start(4, j)
        start(9, j)

    def crossed(j):
        arrived(2, j)
        start(5, j)
        start(6, j)

    def far(j):
        arrived(3, j)
        arrived(4, j)
        start(7, j)

    done = [0, 0, 0, 0]

    def advance(k, upto):
        while done[k] < min(upto + 1, CHUNKS):
            (near, crossed, far, own)[k](done[k])
            done[k] += 1

    def tick(t):
        for k in (0, 1, 3):
            advance(k, t + LEADS[k])

    def stage_c(j):
        if j < CHUNKS:
            for f in (5, 6, 8, 9, 7):
                arrived(f, j)

    def kv_copy(i, received=False):
        buf = (key, val)[i]
        src = (k_hbm, v_hbm)[i].at[pl.ds(HALF, HALF), :]
        dst = buf.at[pl.ds(0, HALF), :]
        return pltpu.make_async_remote_copy(
            src_ref=src, dst_ref=dst, send_sem=kv_send.at[i], recv_sem=kv_recv.at[i],
            device_id=after, device_id_type=MESH,
        )

    def back_copy(i):
        return pltpu.make_async_remote_copy(
            src_ref=(dk_out, dv_out)[i], dst_ref=(dk_in, dv_in)[i],
            send_sem=back_send.at[i], recv_sem=back_recv.at[i],
            device_id=before, device_id_type=MESH,
        )

    loads = [
        pltpu.make_async_copy(k_hbm, key.at[pl.ds(HALF, TOK), :], load.at[0]),
        pltpu.make_async_copy(v_hbm, val.at[pl.ds(HALF, TOK), :], load.at[1]),
        pltpu.make_async_copy(q_hbm, qv, load.at[2]),
        pltpu.make_async_copy(o_hbm, ov, load.at[3]),
        pltpu.make_async_copy(og_hbm, cell(plane, x, 0, TOK), load.at[4]),
        pltpu.make_async_copy(w_hbm, wv, load.at[5]),
    ]
    for c in loads:
        c.start()

    barrier = pltpu.get_barrier_semaphore()
    for d in (right, left, across, after, before):
        pl.semaphore_signal(barrier, inc=1, device_id=d, device_id_type=MESH)
    pl.semaphore_wait(barrier, 5)
    advance(3, LEADS[3] - 3)
    for i in range(2):
        kv_copy(i).start()

    dk_acc[...] = jnp.zeros_like(dk_acc)
    dv_acc[...] = jnp.zeros_like(dv_acc)
    half = ctx * 2
    n_half = n_ctx * 2
    for b in range(3):
        docs = doc_ref[(half + n_half - 1 + b) % n_half].astype(jnp.float32)
        doc_row[:, b * HALF:(b + 1) * HALF] = docs
        doc_col[b * HALF:(b + 1) * HALF, :] = jnp.broadcast_to(docs, (128, HALF)).T

    scale = 1.0 / math.sqrt(HD)

    def span(i):
        r0, n = TILES[i]
        return r0, n, r0 // HALF * HALF, HALF + r0 % HALF + n

    def set_bias(i):
        r0, n, k0, kk = span(i)
        row = doc_row[:, HALF + r0:HALF + r0 + n]
        for lo in range(0, kk, n):
            col = doc_col[k0 + lo:k0 + lo + n, :]
            same = (col if n == 128 else jnp.concatenate([col, col], axis=1)) == row
            if lo + n == kk:
                kp = lax.broadcasted_iota(jnp.int32, (n, n), 0)
                qp = lax.broadcasted_iota(jnp.int32, (n, n), 1)
                same = same & (kp <= qp)
            bias[lo:lo + n, :n] = jnp.where(same, 0.0, -1e30)

    def project(first, n, planes=None, start=True, end=True, at=0):
        def body(hp, carry):
            feats = pl.ds(pl.multiple_of(hp * 2 * HD, 2 * HD), 2 * HD)
            cols = slice(None) if planes is None else pl.ds(pl.multiple_of(planes * (D // 2), D // 2), D // 2)
            got = dot(wv[feats, cols], gat[first:first + n, cols], NT)
            if not start:
                got = part[feats, at:at + n] + got
            if end:
                gt[feats, :n] = got.astype(jnp.bfloat16)
            else:
                part[feats, :n] = got
            return carry

        lax.fori_loop(0, GROUP // 2, body, 0)

    def held(i, h):
        _, n, _, kk = span(i)
        base = GROUP * (0, 768, 1792, 0, 768)[i]
        rows = pl.ds(pl.multiple_of(base + h * kk, 128), kk)
        return (p_wide if n == 256 else p_slim).at[rows, :]

    def weigh(i):
        r0, n, k0, kk = span(i)
        set_bias(i)

        def head(h):
            q = qv[r0:r0 + n, pl.ds(pl.multiple_of(h * HD, HD), HD)]
            lo = r0 // 256 * 256
            lse = lse_ref[pl.ds(h, 1), lo:lo + 256][:, r0 - lo:r0 - lo + n] * LOG2E
            s = dot(key[k0:k0 + kk, :], q, NT)
            p = jnp.exp2((s * (scale * LOG2E) - lse) + bias[:kk, :n])
            held(i, h)[...] = p.astype(jnp.bfloat16)

        def body(hp, carry):
            head(hp * 2)
            head(hp * 2 + 1)
            return carry

        lax.fori_loop(0, GROUP // 2, body, 0)

    def attend(i, first, last):
        r0, n, k0, kk = span(i)

        def head(h):
            c0 = pl.multiple_of(h * HD, HD)
            g = gt[pl.ds(c0, HD), :n]
            q = qv[r0:r0 + n, pl.ds(c0, HD)]
            o = ot[pl.ds(c0, HD), r0:r0 + n]
            delta = jnp.sum(g.astype(jnp.float32) * o.astype(jnp.float32), axis=0, keepdims=True)
            p = held(i, h)[...]
            dp = dot(val[k0:k0 + kk, :], g, NN)
            ds = (p.astype(jnp.float32) * (dp - delta)).astype(jnp.bfloat16)
            dv_acc[k0:k0 + kk, :] += dot(p, g, NT)
            dk_acc[k0:k0 + kk, :] += dot(ds, q, NN)
            dq_t = dot(key_t[:, k0:k0 + kk], ds, NN) * scale
            dq_ref[r0:r0 + n, pl.ds(c0, HD)] = dq_t.T.astype(jnp.bfloat16)

        def body(hp, carry):
            head(hp * 2)
            head(hp * 2 + 1)
            return carry

        lax.fori_loop(first // 2, last // 2, body, 0)

    def out_copy(i):
        r0, n = TILES[i]
        return pltpu.make_async_copy(dq_ref.at[pl.ds(r0, n), :], dq_hbm.at[pl.ds(r0, n), :], store.at[i])

    def back():
        dk_out[...] = dk_acc[:HALF, :].astype(jnp.bfloat16)
        dv_out[...] = dv_acc[:HALF, :].astype(jnp.bfloat16)
        for b in range(2):
            back_copy(b).start()

    def store_rows(i):
        out_copy(i).start()

    for c in (loads[0], loads[1], loads[2]):
        c.wait()
    key_t[:, HALF:] = key[HALF:, :].T
    weigh(2)
    tick(-3)
    weigh(3)
    tick(-2)
    weigh(4)
    advance(2, LEADS[2] - 2)
    loads[3].wait()

    def turn(h, carry):
        c0 = pl.multiple_of(h * HD, HD)
        ot[pl.ds(c0, HD), :] = ov[:, pl.ds(c0, HD)].T
        return carry

    lax.fori_loop(0, GROUP, turn, 0)
    tick(-1)
    for i in range(2):
        kv_copy(i).wait_recv()
    key_t[:, :HALF] = key[:HALF, :].T
    weigh(0)
    advance(2, LEADS[2] - 1)
    weigh(1)
    loads[4].wait()
    loads[5].wait()

    windows = (
        [],
        [(project, 0, 256), (attend, 0, 0, 4)],
        [(attend, 0, 4, 8), (store_rows, 0)],
        [(project, 256, 256), (attend, 1, 0, 4)],
        [(attend, 1, 4, 8), (back,), (store_rows, 1)],
        [(project, 768, 256), (attend, 2, 0, 4), (attend, 2, 4, 8), (store_rows, 2),
         (project, 512, 256, plane, True, False)],
        [(project, 640, 128, other, False, True, 128), (attend, 3, 0, 8), (store_rows, 3)],
        [(project, 512, 128, other, False, True, 0), (attend, 4, 0, 8), (store_rows, 4)],
    )
    for j, work in enumerate(windows):
        stage_c(j)
        tick(j)
        for item in work[:FIRST]:
            item[0](*item[1:])
        advance(2, j + LEADS[2])
        for item in work[FIRST:]:
            item[0](*item[1:])

    for b in range(2):
        back_copy(b).wait()
        kv_copy(b).wait_send()

    for j in range(CHUNKS):
        for f in range(FLOWS):
            if f < 8 or j < EDGED:
                flow(f, j).wait_send()
    dk_ref[:HALF, :] = (dk_acc[HALF:TOK, :] * scale).astype(jnp.bfloat16)
    dk_ref[HALF:, :] = ((dk_acc[TOK:, :] + dk_in[...].astype(jnp.float32)) * scale).astype(jnp.bfloat16)
    dv_ref[:HALF, :] = dv_acc[HALF:TOK, :].astype(jnp.bfloat16)
    dv_ref[HALF:, :] = (dv_acc[TOK:, :] + dv_in[...].astype(jnp.float32)).astype(jnp.bfloat16)
    for i in range(len(TILES)):
        out_copy(i).wait()


def finish(dq, dk, dv, dq_out, dk_out, dv_out, dq_buf, dk_buf, dv_buf, sem_in, sem_out):
    pieces = [(dq.at[pl.ds(r, FROWS), :], dq_buf.at[pl.ds(r, FROWS), :], dq_out.at[pl.ds(r, FROWS), :]) for r in range(0, TOK, FROWS)]
    pieces += [(dk, dk_buf, dk_out), (dv, dv_buf, dv_out)]
    ins = [pltpu.make_async_copy(a, b, sem_in.at[i]) for i, (a, b, _) in enumerate(pieces)]
    outs = [pltpu.make_async_copy(b, c, sem_out.at[i]) for i, (_, b, c) in enumerate(pieces)]
    for c in ins:
        c.start()
    for a, b in zip(ins, outs):
        a.wait()
        b.start()
    for c in outs:
        c.wait()


def per_device(queries, keys, values, outputs, out_grad, out_weight, log_norm, doc_ids):
    bf, f32 = jnp.bfloat16, jnp.float32
    any_ = pl.BlockSpec(memory_space=pl.ANY)
    vm = pl.BlockSpec(memory_space=pltpu.VMEM)
    dma = pltpu.SemaphoreType.DMA
    wide = HALF + TOK
    shapes = (
        jax.ShapeDtypeStruct((TOK, GROUP * HD), bf),
        jax.ShapeDtypeStruct((TOK, HD), bf),
        jax.ShapeDtypeStruct((TOK, HD), bf),
    )
    grads = pl.pallas_call(
        kernel,
        out_shape=shapes,
        in_specs=[any_] * 6 + [vm] * 2,
        out_specs=(any_, vm, vm),
        scratch_shapes=[
            pltpu.VMEM((TOK, GROUP * HD), bf),
            pltpu.VMEM((GROUP * HD, 256), bf),
            pltpu.VMEM((TOK, D), bf),
            pltpu.VMEM((GROUP * HD, D), bf),
            pltpu.VMEM((TOK, GROUP * HD), bf),
            pltpu.VMEM((TOK, GROUP * HD), bf),
            pltpu.VMEM((GROUP * HD, TOK), bf),
            pltpu.VMEM((wide, HD), bf),
            pltpu.VMEM((wide, HD), bf),
            pltpu.VMEM((HD, wide), bf),
            pltpu.VMEM((wide, HD), f32),
            pltpu.VMEM((wide, HD), f32),
            pltpu.VMEM((HALF, HD), bf),
            pltpu.VMEM((HALF, HD), bf),
            pltpu.VMEM((HALF, HD), bf),
            pltpu.VMEM((HALF, HD), bf),
            pltpu.VMEM((GROUP * HD, 256), f32),
            pltpu.VMEM((GROUP * 2816, 256), bf),
            pltpu.VMEM((GROUP * 1408, 128), bf),
            pltpu.VMEM((TOK, 256), f32),
            pltpu.VMEM((wide, 128), f32),
            pltpu.VMEM((1, wide), f32),
            dma((FLOWS, CHUNKS)),
            dma((FLOWS, CHUNKS)),
            dma((2,)), dma((2,)), dma((2,)), dma((2,)), dma((6,)), dma((len(TILES),)),
        ],
        compiler_params=pltpu.CompilerParams(
            collective_id=0, has_side_effects=True, vmem_limit_bytes=58 * 2**20
        ),
        name="attention_backward",
    )(queries, keys, values, outputs, out_grad, out_weight, log_norm, doc_ids.reshape(32, 1, HALF))
    count = TOK // FROWS + 2
    return pl.pallas_call(
        finish, out_shape=shapes, in_specs=[any_] * 3, out_specs=(any_,) * 3, name="results",
        scratch_shapes=[pltpu.VMEM(a.shape, bf) for a in shapes] + [dma((count,)), dma((count,))],
    )(*grads)


def solution(mesh):
    in_specs = (
        P("ctx", "heads"), P("ctx", "heads"), P("ctx", "heads"), P("ctx", "heads"), P("ctx", "heads"),
        P("heads", None), P("heads", "ctx"), P(),
    )
    out_specs = (P("ctx", "heads"), P("ctx", "heads"), P("ctx", "heads"))
    return jax.shard_map(per_device, mesh=mesh, in_specs=in_specs, out_specs=out_specs, check_vma=False)
```

```python
import functools
import math

import jax
import jax.numpy as jnp
from jax import lax
from jax.experimental import pallas as pl
from jax.experimental.pallas import tpu as pltpu
from jax.sharding import PartitionSpec as P

MESH = pl.DeviceIdType.MESH
TOK = 1024
HALF = 512
HD = 128
GROUP = 8
COLS = 640
D = 5120
LEADS = (3, 3, 2, 5)
STARTS = (0, 128, 256, 384, 768, 896, 640, 512)
SIZE = 128
EDGE = 16
TILES = ((0, 256), (256, 256), (768, 256), (512, 256))
FINE = 128 // SIZE
PARTS = tuple((r + k * SIZE, SIZE) for r in STARTS for k in range(FINE))
CHUNKS = len(PARTS)
EDGED = 6
FLOWS = 10
LOG2E = math.log2(math.e)
NT = (((1,), (1,)), ((), ()))
NN = (((1,), (0,)), ((), ()))
FROWS = 256


def dot(a, b, dims):
    return lax.dot_general(a, b, dims, preferred_element_type=jnp.float32)


def kernel(
    q_hbm, k_hbm, v_hbm, o_hbm, og_hbm, w_hbm, lse_ref, doc_ref,
    dq_hbm, dk_ref, dv_ref,
    dq_ref, gt, gat, wv, qv, ov, ot, key, val, key_t, dk_acc, dv_acc, dk_in, dv_in, dk_out, dv_out, part, held, bias, doc_col, doc_row,
    send, recv, kv_send, kv_recv, back_send, back_recv, load, store,
):
    heads = lax.axis_index("heads")
    ctx = lax.axis_index("ctx")
    n_ctx = lax.axis_size("ctx")
    plane, x = heads // 4, heads % 4
    x_left, x_right, x_far = (x + 3) % 4, (x + 1) % 4, (x + 2) % 4
    other = 1 - plane
    right = {"heads": plane * 4 + x_right}
    left = {"heads": plane * 4 + x_left}
    across = {"heads": other * 4 + x}
    after = {"ctx": (ctx + 1) % n_ctx}
    before = {"ctx": (ctx + n_ctx - 1) % n_ctx}

    def cell(pl_, x_, row, rows):
        col = pl.multiple_of((pl_ * 4 + x_) * COLS, 128)
        return gat.at[pl.ds(row, rows), pl.ds(col, COLS)]

    def flow(f, j, received=False):
        r0, rows = PARTS[j]
        low, hr = rows - EDGE * (j < EDGED), rows // 2
        to = (right, left, across, right, left, right, left, across, across, across)[f]
        first, rows = (
            (r0, rows), (r0, rows), (r0, rows), (r0, hr), (r0 + hr, hr),
            (r0, low), (r0, low), (r0, rows), (r0 + low, EDGE), (r0 + low, EDGE),
        )[f]
        sent = (
            (plane, x), (plane, x), (plane, x), (plane, x_left), (plane, x_right),
            (other, x), (other, x), (plane, x_far), (plane, x_left), (plane, x_right),
        )[f]
        filled = (
            (plane, x_left), (plane, x_right), (other, x), (plane, x_far), (plane, x_far),
            (other, x_left), (other, x_right), (other, x_far), (other, x_left), (other, x_right),
        )[f]
        dst = cell(*(filled if received else sent), first, rows)
        src = og_hbm.at[pl.ds(first, rows), :] if f < 3 and not received else dst
        return pltpu.make_async_remote_copy(
            src_ref=src, dst_ref=dst, send_sem=send.at[f, j], recv_sem=recv.at[f, j],
            device_id=to, device_id_type=MESH,
        )

    def start(f, j):
        if f < 8 or j < EDGED:
            flow(f, j).start()

    def arrived(f, j):
        if f < 8 or j < EDGED:
            flow(f, j, received=True).wait_recv()

    def own(j):
        for f in range(3):
            start(f, j)

    def near(j):
        arrived(0, j)
        start(3, j)
        start(8, j)
        arrived(1, j)
        start(4, j)
        start(9, j)

    def crossed(j):
        arrived(2, j)
        start(5, j)
        start(6, j)

    def far(j):
        arrived(3, j)
        arrived(4, j)
        start(7, j)

    done = [0, 0, 0, 0]

    def advance(k, upto):
        while done[k] < min(upto + 1, CHUNKS):
            (near, crossed, far, own)[k](done[k])
            done[k] += 1

    def tick(t):
        for k in (0, 1, 3):
            advance(k, t + LEADS[k])

    def stage_c(j):
        if j < CHUNKS:
            for f in (5, 6, 8, 9, 7):
                arrived(f, j)

    def kv_copy(i, received=False):
        buf = (key, val)[i]
        src = (k_hbm, v_hbm)[i].at[pl.ds(HALF, HALF), :]
        dst = buf.at[pl.ds(0, HALF), :]
        return pltpu.make_async_remote_copy(
            src_ref=src, dst_ref=dst, send_sem=kv_send.at[i], recv_sem=kv_recv.at[i],
            device_id=after, device_id_type=MESH,
        )

    def back_copy(i):
        return pltpu.make_async_remote_copy(
            src_ref=(dk_out, dv_out)[i], dst_ref=(dk_in, dv_in)[i],
            send_sem=back_send.at[i], recv_sem=back_recv.at[i],
            device_id=before, device_id_type=MESH,
        )

    loads = [
        pltpu.make_async_copy(k_hbm, key.at[pl.ds(HALF, TOK), :], load.at[0]),
        pltpu.make_async_copy(v_hbm, val.at[pl.ds(HALF, TOK), :], load.at[1]),
        pltpu.make_async_copy(q_hbm, qv, load.at[2]),
        pltpu.make_async_copy(o_hbm, ov, load.at[3]),
        pltpu.make_async_copy(og_hbm, cell(plane, x, 0, TOK), load.at[4]),
        pltpu.make_async_copy(w_hbm, wv, load.at[5]),
    ]
    for c in loads:
        c.start()

    barrier = pltpu.get_barrier_semaphore()
    for d in (right, left, across, after, before):
        pl.semaphore_signal(barrier, inc=1, device_id=d, device_id_type=MESH)
    pl.semaphore_wait(barrier, 5)
    advance(3, LEADS[3] - 3)
    for i in range(2):
        kv_copy(i).start()

    dk_acc[...] = jnp.zeros_like(dk_acc)
    dv_acc[...] = jnp.zeros_like(dv_acc)
    half = ctx * 2
    n_half = n_ctx * 2
    for b in range(3):
        docs = doc_ref[(half + n_half - 1 + b) % n_half].astype(jnp.float32)
        doc_row[:, b * HALF:(b + 1) * HALF] = docs
        doc_col[b * HALF:(b + 1) * HALF, :] = jnp.broadcast_to(docs, (128, HALF)).T

    scale = 1.0 / math.sqrt(HD)

    def span(i):
        r0, n = TILES[i]
        return r0, n, r0 // HALF * HALF, HALF + r0 % HALF + n

    def set_bias(i):
        r0, n, k0, kk = span(i)
        row = doc_row[:, HALF + r0:HALF + r0 + n]
        for lo in range(0, kk, n):
            col = doc_col[k0 + lo:k0 + lo + n, :]
            same = jnp.concatenate([col, col], axis=1) == row
            if lo + n == kk:
                kp = lax.broadcasted_iota(jnp.int32, (n, n), 0)
                qp = lax.broadcasted_iota(jnp.int32, (n, n), 1)
                same = same & (kp <= qp)
            bias[lo:lo + n, :] = jnp.where(same, 0.0, -1e30)

    def project(i, planes=None):
        r0, n, _, _ = span(i)

        def body(hp, carry):
            feats = pl.ds(pl.multiple_of(hp * 2 * HD, 2 * HD), 2 * HD)
            cols = slice(None) if planes is None else pl.ds(pl.multiple_of(planes * (D // 2), D // 2), D // 2)
            got = dot(wv[feats, cols], gat[r0:r0 + n, cols], NT)
            if planes is plane:
                part[feats, :] = got
            else:
                if planes is other:
                    got = part[feats, :] + got
                gt[feats, :] = got.astype(jnp.bfloat16)
            return carry

        lax.fori_loop(0, GROUP // 2, body, 0)

    def kept(i, h):
        kk = span(i)[3]
        base = GROUP * (0, 768, 1792, 2816)[i]
        return held.at[pl.ds(pl.multiple_of(base + h * kk, 256), kk), :]

    def weigh(i):
        r0, n, k0, kk = span(i)
        set_bias(i)

        def head(h):
            q = qv[r0:r0 + n, pl.ds(pl.multiple_of(h * HD, HD), HD)]
            lse = lse_ref[pl.ds(h, 1), r0:r0 + n] * LOG2E
            s = dot(key[k0:k0 + kk, :], q, NT)
            p = jnp.exp2((s * (scale * LOG2E) - lse) + bias[:kk, :])
            kept(i, h)[...] = p.astype(jnp.bfloat16)

        def body(hp, carry):
            head(hp * 2)
            head(hp * 2 + 1)
            return carry

        lax.fori_loop(0, GROUP // 2, body, 0)

    def attend(i, first, last):
        r0, n, k0, kk = span(i)

        def head(h):
            c0 = pl.multiple_of(h * HD, HD)
            g = gt[pl.ds(c0, HD), :]
            q = qv[r0:r0 + n, pl.ds(c0, HD)]
            o = ot[pl.ds(c0, HD), r0:r0 + n]
            delta = jnp.sum(g.astype(jnp.float32) * o.astype(jnp.float32), axis=0, keepdims=True)
            p = kept(i, h)[...]
            dp = dot(val[k0:k0 + kk, :], g, NN)
            ds = (p.astype(jnp.float32) * (dp - delta)).astype(jnp.bfloat16)
            dv_acc[k0:k0 + kk, :] += dot(p, g, NT)
            dk_acc[k0:k0 + kk, :] += dot(ds, q, NN)
            dq_t = dot(key_t[:, k0:k0 + kk], ds, NN) * scale
            dq_ref[r0:r0 + n, pl.ds(c0, HD)] = dq_t.T.astype(jnp.bfloat16)

        def body(hp, carry):
            head(hp * 2)
            head(hp * 2 + 1)
            return carry

        lax.fori_loop(first // 2, last // 2, body, 0)

    def out_copy(i):
        r0, n = TILES[i]
        return pltpu.make_async_copy(dq_ref.at[pl.ds(r0, n), :], dq_hbm.at[pl.ds(r0, n), :], store.at[i])

    def back():
        dk_out[...] = dk_acc[:HALF, :].astype(jnp.bfloat16)
        dv_out[...] = dv_acc[:HALF, :].astype(jnp.bfloat16)
        for b in range(2):
            back_copy(b).start()

    def store_rows(i):
        out_copy(i).start()

    for c in (loads[0], loads[1], loads[2]):
        c.wait()
    key_t[:, HALF:] = key[HALF:, :].T
    weigh(2)
    tick(-3)
    weigh(3)
    tick(-2)
    advance(2, LEADS[2] - 2)
    loads[3].wait()

    def turn(h, carry):
        c0 = pl.multiple_of(h * HD, HD)
        ot[pl.ds(c0, HD), :] = ov[:, pl.ds(c0, HD)].T
        return carry

    lax.fori_loop(0, GROUP, turn, 0)
    tick(-1)
    for i in range(2):
        kv_copy(i).wait_recv()
    key_t[:, :HALF] = key[:HALF, :].T
    weigh(0)
    advance(2, LEADS[2] - 1)
    weigh(1)
    loads[4].wait()
    loads[5].wait()

    windows = {
        1: [(project, 0), (attend, 0, 0, 4)],
        2: [(attend, 0, 4, 8), (store_rows, 0)],
        3: [(project, 1), (attend, 1, 0, 4)],
        4: [(attend, 1, 4, 8), (back,), (store_rows, 1)],
        5: [(project, 2), (attend, 2, 0, 4), (attend, 2, 4, 8), (store_rows, 2), (project, 3, plane)],
        7: [(project, 3, other), (attend, 3, 0, 8), (store_rows, 3)],
    }
    for j in range(CHUNKS):
        stage_c(j)
        tick(j)
        work = windows.get((j + 1) // FINE - 1, []) if (j + 1) % FINE == 0 else []
        for item in work[:1]:
            item[0](*item[1:])
        advance(2, j + LEADS[2])
        for item in work[1:]:
            item[0](*item[1:])

    for b in range(2):
        back_copy(b).wait()
        kv_copy(b).wait_send()

    for j in range(CHUNKS):
        for f in range(FLOWS):
            if f < 8 or j < EDGED:
                flow(f, j).wait_send()
    dk_ref[:HALF, :] = (dk_acc[HALF:TOK, :] * scale).astype(jnp.bfloat16)
    dk_ref[HALF:, :] = ((dk_acc[TOK:, :] + dk_in[...].astype(jnp.float32)) * scale).astype(jnp.bfloat16)
    dv_ref[:HALF, :] = dv_acc[HALF:TOK, :].astype(jnp.bfloat16)
    dv_ref[HALF:, :] = (dv_acc[TOK:, :] + dv_in[...].astype(jnp.float32)).astype(jnp.bfloat16)
    for i in range(len(TILES)):
        out_copy(i).wait()


def finish(dq, dk, dv, dq_out, dk_out, dv_out, dq_buf, dk_buf, dv_buf, sem_in, sem_out):
    pieces = [(dq.at[pl.ds(r, FROWS), :], dq_buf.at[pl.ds(r, FROWS), :], dq_out.at[pl.ds(r, FROWS), :]) for r in range(0, TOK, FROWS)]
    pieces += [(dk, dk_buf, dk_out), (dv, dv_buf, dv_out)]
    ins = [pltpu.make_async_copy(a, b, sem_in.at[i]) for i, (a, b, _) in enumerate(pieces)]
    outs = [pltpu.make_async_copy(b, c, sem_out.at[i]) for i, (_, b, c) in enumerate(pieces)]
    for c in ins:
        c.start()
    for a, b in zip(ins, outs):
        a.wait()
        b.start()
    for c in outs:
        c.wait()


def per_device(queries, keys, values, outputs, out_grad, out_weight, log_norm, doc_ids):
    bf, f32 = jnp.bfloat16, jnp.float32
    any_ = pl.BlockSpec(memory_space=pl.ANY)
    vm = pl.BlockSpec(memory_space=pltpu.VMEM)
    dma = pltpu.SemaphoreType.DMA
    wide = HALF + TOK
    shapes = (
        jax.ShapeDtypeStruct((TOK, GROUP * HD), bf),
        jax.ShapeDtypeStruct((TOK, HD), bf),
        jax.ShapeDtypeStruct((TOK, HD), bf),
    )
    grads = pl.pallas_call(
        kernel,
        out_shape=shapes,
        in_specs=[any_] * 6 + [vm] * 2,
        out_specs=(any_, vm, vm),
        scratch_shapes=[
            pltpu.VMEM((TOK, GROUP * HD), bf),
            pltpu.VMEM((GROUP * HD, 256), bf),
            pltpu.VMEM((TOK, D), bf),
            pltpu.VMEM((GROUP * HD, D), bf),
            pltpu.VMEM((TOK, GROUP * HD), bf),
            pltpu.VMEM((TOK, GROUP * HD), bf),
            pltpu.VMEM((GROUP * HD, TOK), bf),
            pltpu.VMEM((wide, HD), bf),
            pltpu.VMEM((wide, HD), bf),
            pltpu.VMEM((HD, wide), bf),
            pltpu.VMEM((wide, HD), f32),
            pltpu.VMEM((wide, HD), f32),
            pltpu.VMEM((HALF, HD), bf),
            pltpu.VMEM((HALF, HD), bf),
            pltpu.VMEM((HALF, HD), bf),
            pltpu.VMEM((HALF, HD), bf),
            pltpu.VMEM((GROUP * HD, 256), f32),
            pltpu.VMEM((GROUP * 3584, 256), bf),
            pltpu.VMEM((TOK, 256), f32),
            pltpu.VMEM((wide, 128), f32),
            pltpu.VMEM((1, wide), f32),
            dma((FLOWS, CHUNKS)),
            dma((FLOWS, CHUNKS)),
            dma((2,)), dma((2,)), dma((2,)), dma((2,)), dma((6,)), dma((len(TILES),)),
        ],
        compiler_params=pltpu.CompilerParams(
            collective_id=0, has_side_effects=True, vmem_limit_bytes=58 * 2**20
        ),
        name="attention_backward",
    )(queries, keys, values, outputs, out_grad, out_weight, log_norm, doc_ids.reshape(32, 1, HALF))
    count = TOK // FROWS + 2
    return pl.pallas_call(
        finish, out_shape=shapes, in_specs=[any_] * 3, out_specs=(any_,) * 3, name="results",
        scratch_shapes=[pltpu.VMEM(a.shape, bf) for a in shapes] + [dma((count,)), dma((count,))],
    )(*grads)


def solution(mesh):
    in_specs = (
        P("ctx", "heads"), P("ctx", "heads"), P("ctx", "heads"), P("ctx", "heads"), P("ctx", "heads"),
        P("heads", None), P("heads", "ctx"), P(),
    )
    out_specs = (P("ctx", "heads"), P("ctx", "heads"), P("ctx", "heads"))
    return jax.shard_map(per_device, mesh=mesh, in_specs=in_specs, out_specs=out_specs, check_vma=False)
```

```python
import functools
import math

import jax
import jax.numpy as jnp
from jax import lax
from jax.experimental import pallas as pl
from jax.experimental.pallas import tpu as pltpu
from jax.sharding import PartitionSpec as P

MESH = pl.DeviceIdType.MESH
TOK = 1024
HALF = 512
HD = 128
GROUP = 8
COLS = 640
D = 5120
LEADS = (3, 3, 2, 5)
STARTS = (0, 128, 256, 384, 768, 896, 640, 512)
SIZE = 128
EDGE = 16
TILES = ((0, 256), (256, 256), (768, 256), (512, 256))
FINE = 128 // SIZE
PARTS = tuple((r + k * SIZE, SIZE) for r in STARTS for k in range(FINE))
CHUNKS = len(PARTS)
EDGED = 6
FLOWS = 10
LOG2E = math.log2(math.e)
NT = (((1,), (1,)), ((), ()))
NN = (((1,), (0,)), ((), ()))
FROWS = 256


def dot(a, b, dims):
    return lax.dot_general(a, b, dims, preferred_element_type=jnp.float32)


def kernel(
    q_hbm, k_hbm, v_hbm, o_hbm, og_hbm, w_hbm, lse_ref, doc_ref,
    dq_hbm, dk_ref, dv_ref,
    dq_ref, gt, gat, wv, qv, ov, ot, key, val, key_t, dk_acc, dv_acc, dk_in, dv_in, dk_out, dv_out, part, held, bias, doc_col, doc_row,
    send, recv, kv_send, kv_recv, back_send, back_recv, load, store,
):
    heads = lax.axis_index("heads")
    ctx = lax.axis_index("ctx")
    n_ctx = lax.axis_size("ctx")
    plane, x = heads // 4, heads % 4
    x_left, x_right, x_far = (x + 3) % 4, (x + 1) % 4, (x + 2) % 4
    other = 1 - plane
    right = {"heads": plane * 4 + x_right}
    left = {"heads": plane * 4 + x_left}
    across = {"heads": other * 4 + x}
    after = {"ctx": (ctx + 1) % n_ctx}
    before = {"ctx": (ctx + n_ctx - 1) % n_ctx}

    def cell(pl_, x_, row, rows):
        col = pl.multiple_of((pl_ * 4 + x_) * COLS, 128)
        return gat.at[pl.ds(row, rows), pl.ds(col, COLS)]

    def flow(f, j, received=False):
        r0, rows = PARTS[j]
        low, hr = rows - EDGE * (j < EDGED), rows // 2
        to = (right, left, across, right, left, right, left, across, across, across)[f]
        first, rows = (
            (r0, rows), (r0, rows), (r0, rows), (r0, hr), (r0 + hr, hr),
            (r0, low), (r0, low), (r0, rows), (r0 + low, EDGE), (r0 + low, EDGE),
        )[f]
        sent = (
            (plane, x), (plane, x), (plane, x), (plane, x_left), (plane, x_right),
            (other, x), (other, x), (plane, x_far), (plane, x_left), (plane, x_right),
        )[f]
        filled = (
            (plane, x_left), (plane, x_right), (other, x), (plane, x_far), (plane, x_far),
            (other, x_left), (other, x_right), (other, x_far), (other, x_left), (other, x_right),
        )[f]
        dst = cell(*(filled if received else sent), first, rows)
        src = og_hbm.at[pl.ds(first, rows), :] if f < 3 and not received else dst
        return pltpu.make_async_remote_copy(
            src_ref=src, dst_ref=dst, send_sem=send.at[f, j], recv_sem=recv.at[f, j],
            device_id=to, device_id_type=MESH,
        )

    def start(f, j):
        if f < 8 or j < EDGED:
            flow(f, j).start()

    def arrived(f, j):
        if f < 8 or j < EDGED:
            flow(f, j, received=True).wait_recv()

    def own(j):
        for f in range(3):
            start(f, j)

    def near(j):
        arrived(0, j)
        start(3, j)
        start(8, j)
        arrived(1, j)
        start(4, j)
        start(9, j)

    def crossed(j):
        arrived(2, j)
        start(5, j)
        start(6, j)

    def far(j):
        arrived(3, j)
        arrived(4, j)
        start(7, j)

    done = [0, 0, 0, 0]

    def advance(k, upto):
        while done[k] < min(upto + 1, CHUNKS):
            (near, crossed, far, own)[k](done[k])
            done[k] += 1

    def tick(t):
        for k in (0, 1, 3):
            advance(k, t + LEADS[k])

    def stage_c(j):
        if j < CHUNKS:
            for f in (5, 6, 8, 9, 7):
                arrived(f, j)

    def kv_copy(i, received=False):
        buf = (key, val)[i]
        src = (k_hbm, v_hbm)[i].at[pl.ds(HALF, HALF), :]
        dst = buf.at[pl.ds(0, HALF), :]
        return pltpu.make_async_remote_copy(
            src_ref=src, dst_ref=dst, send_sem=kv_send.at[i], recv_sem=kv_recv.at[i],
            device_id=after, device_id_type=MESH,
        )

    def back_copy(i):
        return pltpu.make_async_remote_copy(
            src_ref=(dk_out, dv_out)[i], dst_ref=(dk_in, dv_in)[i],
            send_sem=back_send.at[i], recv_sem=back_recv.at[i],
            device_id=before, device_id_type=MESH,
        )

    loads = [
        pltpu.make_async_copy(k_hbm, key.at[pl.ds(HALF, TOK), :], load.at[0]),
        pltpu.make_async_copy(v_hbm, val.at[pl.ds(HALF, TOK), :], load.at[1]),
        pltpu.make_async_copy(q_hbm, qv, load.at[2]),
        pltpu.make_async_copy(o_hbm, ov, load.at[3]),
        pltpu.make_async_copy(og_hbm, cell(plane, x, 0, TOK), load.at[4]),
        pltpu.make_async_copy(w_hbm, wv, load.at[5]),
    ]
    for c in loads:
        c.start()

    barrier = pltpu.get_barrier_semaphore()
    for d in (right, left, across, after, before):
        pl.semaphore_signal(barrier, inc=1, device_id=d, device_id_type=MESH)
    pl.semaphore_wait(barrier, 5)
    advance(3, LEADS[3] - 3)
    for i in range(2):
        kv_copy(i).start()

    dk_acc[...] = jnp.zeros_like(dk_acc)
    dv_acc[...] = jnp.zeros_like(dv_acc)
    half = ctx * 2
    n_half = n_ctx * 2
    for b in range(3):
        docs = doc_ref[(half + n_half - 1 + b) % n_half].astype(jnp.float32)
        doc_row[:, b * HALF:(b + 1) * HALF] = docs
        doc_col[b * HALF:(b + 1) * HALF, :] = jnp.broadcast_to(docs, (128, HALF)).T

    scale = 1.0 / math.sqrt(HD)

    def span(i):
        r0, n = TILES[i]
        return r0, n, r0 // HALF * HALF, HALF + r0 % HALF + n

    def set_bias(i):
        r0, n, k0, kk = span(i)
        row = doc_row[:, HALF + r0:HALF + r0 + n]
        for lo in range(0, kk, n):
            col = doc_col[k0 + lo:k0 + lo + n, :]
            same = jnp.concatenate([col, col], axis=1) == row
            if lo + n == kk:
                kp = lax.broadcasted_iota(jnp.int32, (n, n), 0)
                qp = lax.broadcasted_iota(jnp.int32, (n, n), 1)
                same = same & (kp <= qp)
            bias[lo:lo + n, :] = jnp.where(same, 0.0, -1e30)

    def project(i, planes=None):
        r0, n, _, _ = span(i)

        def body(hp, carry):
            feats = pl.ds(pl.multiple_of(hp * 2 * HD, 2 * HD), 2 * HD)
            cols = slice(None) if planes is None else pl.ds(pl.multiple_of(planes * (D // 2), D // 2), D // 2)
            got = dot(wv[feats, cols], gat[r0:r0 + n, cols], NT)
            if planes is plane:
                part[feats, :] = got
            else:
                if planes is other:
                    got = part[feats, :] + got
                gt[feats, :] = got.astype(jnp.bfloat16)
            return carry

        lax.fori_loop(0, GROUP // 2, body, 0)

    def kept(i, h):
        kk = span(i)[3]
        base = GROUP * (0, 768, 1792, 2816)[i]
        return held.at[pl.ds(pl.multiple_of(base + h * kk, 256), kk), :]

    def weigh(i):
        r0, n, k0, kk = span(i)
        set_bias(i)

        def head(h):
            q = qv[r0:r0 + n, pl.ds(pl.multiple_of(h * HD, HD), HD)]
            lse = lse_ref[pl.ds(h, 1), r0:r0 + n] * LOG2E
            s = dot(key[k0:k0 + kk, :], q, NT)
            p = jnp.exp2((s * (scale * LOG2E) - lse) + bias[:kk, :])
            kept(i, h)[...] = p.astype(jnp.bfloat16)

        def body(hp, carry):
            head(hp * 2)
            head(hp * 2 + 1)
            return carry

        lax.fori_loop(0, GROUP // 2, body, 0)

    def attend(i, first, last):
        r0, n, k0, kk = span(i)

        def head(h):
            c0 = pl.multiple_of(h * HD, HD)
            g = gt[pl.ds(c0, HD), :]
            q = qv[r0:r0 + n, pl.ds(c0, HD)]
            o = ot[pl.ds(c0, HD), r0:r0 + n]
            delta = jnp.sum(g.astype(jnp.float32) * o.astype(jnp.float32), axis=0, keepdims=True)
            p = kept(i, h)[...]
            dp = dot(val[k0:k0 + kk, :], g, NN)
            ds = (p.astype(jnp.float32) * (dp - delta)).astype(jnp.bfloat16)
            dv_acc[k0:k0 + kk, :] += dot(p, g, NT)
            dk_acc[k0:k0 + kk, :] += dot(ds, q, NN)
            dq_t = dot(key_t[:, k0:k0 + kk], ds, NN) * scale
            dq_ref[r0:r0 + n, pl.ds(c0, HD)] = dq_t.T.astype(jnp.bfloat16)

        def body(hp, carry):
            head(hp * 2)
            head(hp * 2 + 1)
            return carry

        lax.fori_loop(first // 2, last // 2, body, 0)

    def out_copy(i):
        r0, n = TILES[i]
        return pltpu.make_async_copy(dq_ref.at[pl.ds(r0, n), :], dq_hbm.at[pl.ds(r0, n), :], store.at[i])

    def back():
        dk_out[...] = dk_acc[:HALF, :].astype(jnp.bfloat16)
        dv_out[...] = dv_acc[:HALF, :].astype(jnp.bfloat16)
        for b in range(2):
            back_copy(b).start()

    def store_rows(i):
        out_copy(i).start()

    for c in (loads[0], loads[1], loads[2]):
        c.wait()
    key_t[:, HALF:] = key[HALF:, :].T
    weigh(2)
    tick(-3)
    weigh(3)
    tick(-2)
    advance(2, LEADS[2] - 2)
    loads[3].wait()

    def turn(h, carry):
        c0 = pl.multiple_of(h * HD, HD)
        ot[pl.ds(c0, HD), :] = ov[:, pl.ds(c0, HD)].T
        return carry

    lax.fori_loop(0, GROUP, turn, 0)
    tick(-1)
    for i in range(2):
        kv_copy(i).wait_recv()
    key_t[:, :HALF] = key[:HALF, :].T
    weigh(0)
    advance(2, LEADS[2] - 1)
    weigh(1)
    loads[4].wait()
    loads[5].wait()

    windows = {
        1: [(project, 0), (attend, 0, 0, 4)],
        2: [(attend, 0, 4, 8), (store_rows, 0)],
        3: [(project, 1), (attend, 1, 0, 4)],
        4: [(attend, 1, 4, 8), (back,), (store_rows, 1)],
        5: [(project, 2), (attend, 2, 0, 4), (attend, 2, 4, 8), (store_rows, 2), (project, 3, plane)],
        7: [(project, 3, other), (attend, 3, 0, 8), (store_rows, 3)],
    }
    for j in range(CHUNKS):
        stage_c(j)
        tick(j)
        work = windows.get((j + 1) // FINE - 1, []) if (j + 1) % FINE == 0 else []
        ahead = 3 if j == 5 else 1
        for item in work[:ahead]:
            item[0](*item[1:])
        advance(2, j + LEADS[2])
        for item in work[ahead:]:
            item[0](*item[1:])

    for b in range(2):
        back_copy(b).wait()
        kv_copy(b).wait_send()

    for j in range(CHUNKS):
        for f in range(FLOWS):
            if f < 8 or j < EDGED:
                flow(f, j).wait_send()
    dk_ref[:HALF, :] = (dk_acc[HALF:TOK, :] * scale).astype(jnp.bfloat16)
    dk_ref[HALF:, :] = ((dk_acc[TOK:, :] + dk_in[...].astype(jnp.float32)) * scale).astype(jnp.bfloat16)
    dv_ref[:HALF, :] = dv_acc[HALF:TOK, :].astype(jnp.bfloat16)
    dv_ref[HALF:, :] = (dv_acc[TOK:, :] + dv_in[...].astype(jnp.float32)).astype(jnp.bfloat16)
    for i in range(len(TILES)):
        out_copy(i).wait()


def finish(dq, dk, dv, dq_out, dk_out, dv_out, dq_buf, dk_buf, dv_buf, sem_in, sem_out):
    pieces = [(dq.at[pl.ds(r, FROWS), :], dq_buf.at[pl.ds(r, FROWS), :], dq_out.at[pl.ds(r, FROWS), :]) for r in range(0, TOK, FROWS)]
    pieces += [(dk, dk_buf, dk_out), (dv, dv_buf, dv_out)]
    ins = [pltpu.make_async_copy(a, b, sem_in.at[i]) for i, (a, b, _) in enumerate(pieces)]
    outs = [pltpu.make_async_copy(b, c, sem_out.at[i]) for i, (_, b, c) in enumerate(pieces)]
    for c in ins:
        c.start()
    for a, b in zip(ins, outs):
        a.wait()
        b.start()
    for c in outs:
        c.wait()


def per_device(queries, keys, values, outputs, out_grad, out_weight, log_norm, doc_ids):
    bf, f32 = jnp.bfloat16, jnp.float32
    any_ = pl.BlockSpec(memory_space=pl.ANY)
    vm = pl.BlockSpec(memory_space=pltpu.VMEM)
    dma = pltpu.SemaphoreType.DMA
    wide = HALF + TOK
    shapes = (
        jax.ShapeDtypeStruct((TOK, GROUP * HD), bf),
        jax.ShapeDtypeStruct((TOK, HD), bf),
        jax.ShapeDtypeStruct((TOK, HD), bf),
    )
    grads = pl.pallas_call(
        kernel,
        out_shape=shapes,
        in_specs=[any_] * 6 + [vm] * 2,
        out_specs=(any_, vm, vm),
        scratch_shapes=[
            pltpu.VMEM((TOK, GROUP * HD), bf),
            pltpu.VMEM((GROUP * HD, 256), bf),
            pltpu.VMEM((TOK, D), bf),
            pltpu.VMEM((GROUP * HD, D), bf),
            pltpu.VMEM((TOK, GROUP * HD), bf),
            pltpu.VMEM((TOK, GROUP * HD), bf),
            pltpu.VMEM((GROUP * HD, TOK), bf),
            pltpu.VMEM((wide, HD), bf),
            pltpu.VMEM((wide, HD), bf),
            pltpu.VMEM((HD, wide), bf),
            pltpu.VMEM((wide, HD), f32),
            pltpu.VMEM((wide, HD), f32),
            pltpu.VMEM((HALF, HD), bf),
            pltpu.VMEM((HALF, HD), bf),
            pltpu.VMEM((HALF, HD), bf),
            pltpu.VMEM((HALF, HD), bf),
            pltpu.VMEM((GROUP * HD, 256), f32),
            pltpu.VMEM((GROUP * 3584, 256), bf),
            pltpu.VMEM((TOK, 256), f32),
            pltpu.VMEM((wide, 128), f32),
            pltpu.VMEM((1, wide), f32),
            dma((FLOWS, CHUNKS)),
            dma((FLOWS, CHUNKS)),
            dma((2,)), dma((2,)), dma((2,)), dma((2,)), dma((6,)), dma((len(TILES),)),
        ],
        compiler_params=pltpu.CompilerParams(
            collective_id=0, has_side_effects=True, vmem_limit_bytes=58 * 2**20
        ),
        name="attention_backward",
    )(queries, keys, values, outputs, out_grad, out_weight, log_norm, doc_ids.reshape(32, 1, HALF))
    count = TOK // FROWS + 2
    return pl.pallas_call(
        finish, out_shape=shapes, in_specs=[any_] * 3, out_specs=(any_,) * 3, name="results",
        scratch_shapes=[pltpu.VMEM(a.shape, bf) for a in shapes] + [dma((count,)), dma((count,))],
    )(*grads)


def solution(mesh):
    in_specs = (
        P("ctx", "heads"), P("ctx", "heads"), P("ctx", "heads"), P("ctx", "heads"), P("ctx", "heads"),
        P("heads", None), P("heads", "ctx"), P(),
    )
    out_specs = (P("ctx", "heads"), P("ctx", "heads"), P("ctx", "heads"))
    return jax.shard_map(per_device, mesh=mesh, in_specs=in_specs, out_specs=out_specs, check_vma=False)
```
